32 devices in a mesh: rec: 16 (over z, y, core), feat: 2 (over x).
Axes of the slice: x: 2, y: 2, z: 4, core: 2. Of those that a mesh axis runs over, the one named last changes fastest.
Arguments:
- real_profiles: bfloat16 [8192, 10240], P('rec', 'feat'), may hold values from -4 to 4
- synthetic_profiles: bfloat16 [1024, 10240], P('rec', 'feat'), may hold values from -10 to 10
- projection: bfloat16 [10240, 512], P('feat'), may hold values from -0.0625 to 0.0625
Outputs:
- real_min: float32 [8192], P('rec')
- synthetic_min: float32 [1024], P('rec')
The draws below stay inside these ranges and needn't reach their ends.
All inputs are finite; a program needn't handle non-finite values.
Results may differ from the reference program's by a relative error of at most 0.0003.
Values sent between devices are 32-bit elements; how exact they have to be, the bound alone decides.
A program may use at most 64 MiB of HBM per device.

```python
import jax
import jax.numpy as jnp
from jax import lax

K = 512
G = 10240
RDR = 512
RDS = 64
NR = 8192
NS = 1024
N_REC = 16


def single_profile(base_key, position):
    sample_key = jax.random.fold_in(base_key, position)
    values = jax.random.truncated_normal(sample_key, -4.0, 4.0, (G,), jnp.float32)
    return values


def draw_real_profiles(key, part):
    base_key = jax.random.fold_in(key, 11)
    positions = jnp.arange(NR, dtype=jnp.int32).reshape(-1, RDR)

    def make_block(block_positions):
        return jax.vmap(lambda position: single_profile(base_key, position))(block_positions).astype(jnp.bfloat16)
    return lax.map(make_block, positions).reshape(NR, G)


def draw_synthetic_profiles(key, part):
    base_key = jax.random.fold_in(key, 11)
    sources = jax.random.randint(jax.random.fold_in(key, 12), (NS,), 0, NR)
    noise_key = jax.random.fold_in(key, 13)
    spread_key = jax.random.fold_in(key, 14)

    def single_synthetic(position, source):
        initial = single_profile(base_key, source)
        noise_values = jax.random.truncated_normal(jax.random.fold_in(noise_key, position), -4.0, 4.0, (G,), jnp.float32)
        spread = jnp.exp(jax.random.uniform(jax.random.fold_in(spread_key, position), (), jnp.float32, jnp.log(0.1), jnp.log(1.5)))
        return initial + spread * noise_values
    positions = jnp.arange(NS, dtype=jnp.int32).reshape(-1, RDS)
    source_blocks = sources.reshape(-1, RDS)

    def make_block(inputs):
        block_positions, block_sources = inputs
        return jax.vmap(single_synthetic)(block_positions, block_sources).astype(jnp.bfloat16)
    return lax.map(make_block, (positions, source_blocks)).reshape(NS, G)


def block_scale(own_key, extent, shards, low, high):
    level, own = 1.0, jax.random.fold_in(own_key, 6)
    for dim, blocks in shards:
        draws = jnp.exp(jax.random.uniform(jax.random.fold_in(own, dim), (blocks,), jnp.float32, low / len(shards), high / len(shards)))
        level = level * jnp.repeat(draws, extent[dim] // blocks).reshape([-1 if axis == dim else 1 for axis in range(len(extent))])
    return level


def centred(rng, dims, scale, most, split=(), kind=jnp.bfloat16):
    gain = block_scale(rng, dims, split, -0.22, 0.18) if split else 1.0
    drawn = jax.random.normal(rng, dims, jnp.float32) * scale * gain
    return jnp.minimum(jnp.maximum(drawn, -most), most).astype(kind)


def setup_inputs(seed: int = 0) -> dict:
    streams_of = jax.random.split(jax.random.key(seed), 4)
    return {
        "real_profiles": draw_real_profiles(jax.random.fold_in(streams_of[3], 71), 0),
        "synthetic_profiles": draw_synthetic_profiles(jax.random.fold_in(streams_of[3], 71), 0),
        "projection": centred(streams_of[2], (G, K), G ** -0.5, 0.0625, ((0, 2),)),
    }


def reference(real_profiles, synthetic_profiles, projection):
    real_embed = jnp.dot(real_profiles, projection, preferred_element_type=jnp.float32)
    synth_embed = jnp.dot(synthetic_profiles, projection, preferred_element_type=jnp.float32)
    real_norm = jnp.sum(jnp.square(real_embed), axis=1)
    synth_norm = jnp.sum(jnp.square(synth_embed), axis=1)
    embed_blocks = synth_embed.reshape(N_REC, RDS, K)
    norm_blocks = synth_norm.reshape(N_REC, RDS)

    def one_block(best_real, inputs):
        block_embed, block_norm = inputs
        products = lax.dot_general(block_embed, real_embed, (((1,), (1,)), ((), ())), precision=lax.Precision.HIGHEST, preferred_element_type=jnp.float32)
        distance = block_norm[:, None] + real_norm[None, :] - 2.0 * products
        return jnp.minimum(best_real, jnp.min(distance, axis=0)), jnp.min(distance, axis=1)

    start_min = jnp.full((N_REC * RDR,), jnp.inf, jnp.float32)
    best_real, synth_mins = lax.scan(one_block, start_min, (embed_blocks, norm_blocks))
    return best_real / K, synth_mins.reshape(N_REC * RDS) / K
```

```python
import functools

import jax
import jax.numpy as jnp
from jax import lax
from jax.experimental import pallas as pl
from jax.experimental.pallas import tpu as pltpu
from jax.sharding import PartitionSpec as P

MESH = pl.DeviceIdType.MESH
UP_Z, DOWN_Z, UP_Y, DOWN_Y, CORE = range(5)


def split(x):
    hi = x.astype(jnp.bfloat16)
    lo = (x - hi.astype(jnp.float32)).astype(jnp.bfloat16)
    return hi, lo


def kernel(
    n_rec, n_feat, n_z, n_y, n_k,
    real_hbm, synth_hbm, proj_hbm, out_real, out_synth,
    x_v, proj_v, part, s_recv, r_recv, s_all, s_cat, s_norm, min_send, min_recv, rmin,
    in_sem, rest_sem, sx_send, sx_recv, rx_send, rx_recv, g_send, g_recv,
    m_send, m_recv, o_send, o_recv,
):
    r = lax.axis_index("rec")
    f = lax.axis_index("feat")
    c = lax.rem(r, 2)
    chip = r // 2
    y = lax.rem(chip, n_y)
    z = chip // n_y
    n_dev = n_rec * n_feat
    me = r * n_feat + f
    rows_s, genes = synth_hbm.shape
    rows_r = real_hbm.shape[0]
    width = proj_hbm.shape[1]
    own = rows_r // n_feat
    step = genes // n_k

    def chunk(q):
        start = lax.rem(f + q, n_feat) * own
        return pl.ds(pl.multiple_of(start, own), own)

    def x_rows(q):
        return pl.ds(rows_s + (q - 1) * own, own)

    loads = []
    for k in range(n_k):
        ks = pl.ds(k * step, step)
        loads.append([
            pltpu.make_async_copy(proj_hbm.at[ks], proj_v.at[ks], in_sem.at[k, 0]),
            pltpu.make_async_copy(synth_hbm.at[:, ks], x_v.at[pl.ds(0, rows_s), ks], in_sem.at[k, 1]),
            pltpu.make_async_copy(real_hbm.at[chunk(1), ks], x_v.at[x_rows(1), ks], in_sem.at[k, 2]),
        ])
        for copy in loads[-1]:
            copy.start()
    rest = []
    for q in range(2, n_feat + 1):
        rest.append(pltpu.make_async_copy(real_hbm.at[chunk(q)], x_v.at[x_rows(q)], rest_sem.at[q - 2]))
        rest[-1].start()

    barrier = pltpu.get_barrier_semaphore()

    def greet(i, carry):
        peer = lax.rem(me + i, n_dev)
        pl.semaphore_signal(
            barrier, inc=1, device_id=(peer // n_feat, lax.rem(peer, n_feat)), device_id_type=MESH
        )
        return carry

    lax.fori_loop(1, n_dev, greet, 0)

    head = rows_s + own
    for k in range(n_k):
        for copy in loads[k]:
            copy.wait()
        ks = pl.ds(k * step, step)
        term = jnp.dot(x_v[0:head, ks], proj_v[ks, :], preferred_element_type=jnp.float32)
        if k == 0:
            part[0:head, :] = term
        else:
            part[0:head, :] += term
    pl.semaphore_wait(barrier, n_dev - 1)

    s_copies, r_copies = [], []
    for q in range(1, n_feat):
        to = (r, lax.rem(f + q, n_feat))
        s_copies.append(pltpu.make_async_remote_copy(
            src_ref=part.at[pl.ds(0, rows_s)], dst_ref=s_recv.at[q - 1],
            send_sem=sx_send.at[q - 1], recv_sem=sx_recv.at[q - 1],
            device_id=to, device_id_type=MESH,
        ))
        r_copies.append(pltpu.make_async_remote_copy(
            src_ref=part.at[x_rows(q)], dst_ref=r_recv.at[q - 1],
            send_sem=rx_send.at[q - 1], recv_sem=rx_recv.at[q - 1],
            device_id=to, device_id_type=MESH,
        ))
        s_copies[-1].start()
    for q in range(2, n_feat + 1):
        rest[q - 2].wait()
        part[x_rows(q), :] = jnp.dot(x_v[x_rows(q), :], proj_v[...], preferred_element_type=jnp.float32)
    for copy in s_copies:
        copy.wait_send()
    for copy in r_copies:
        copy.start()

    def index(zz, yy, cc):
        return (zz * n_y + yy) * 2 + cc

    def forward(piece, slot):
        to = {
            UP_Z: index(z + 1, y, c), DOWN_Z: index(z - 1, y, c),
            UP_Y: index(z, y + 1, c), DOWN_Y: index(z, y - 1, c), CORE: index(z, y, 1 - c),
        }[slot]
        return pltpu.make_async_remote_copy(
            src_ref=s_all.at[piece], dst_ref=s_all.at[piece],
            send_sem=g_send.at[piece, slot], recv_sem=g_recv.at[piece],
            device_id=(to, f), device_id_type=MESH,
        )

    exists = {UP_Z: z + 1 < n_z, DOWN_Z: z > 0, UP_Y: y + 1 < n_y, DOWN_Y: y > 0}
    sends = []

    def send(piece, slot, when):
        if slot in exists:
            when = exists[slot] if when is None else jnp.logical_and(when, exists[slot])
        sends.append((piece, slot, when))
        if when is None:
            forward(piece, slot).start()
        else:
            pl.when(when)(lambda: forward(piece, slot).start())

    for copy in s_copies:
        copy.wait_recv()
    total = part[0:rows_s, :]
    for q in range(1, n_feat):
        total = total + s_recv[q - 1]
    s_all[r] = total
    for slot in (UP_Z, DOWN_Z, UP_Y, DOWN_Y, CORE):
        send(r, slot, None)

    def arrived(piece, when):
        pl.when(when)(lambda: forward(piece, CORE).wait_recv())

    for d in range(1, n_z):
        for way in (1, -1):
            zs = z - way * d
            here = zs >= 0 if way > 0 else zs < n_z
            piece = index(zs, y, c)
            arrived(piece, here)
            send(piece, UP_Z if way > 0 else DOWN_Z, here)
            for slot in (UP_Y, DOWN_Y, CORE):
                send(piece, slot, here)
    for d in range(1, n_y):
        for zd in range(n_z):
            for zway in (1, -1)[: 2 if zd else 1]:
                zs = z - zway * zd
                z_ok = zs >= 0 if zway > 0 else zs < n_z
                for way in (1, -1):
                    ys = y - way * d
                    here = jnp.logical_and(z_ok, ys >= 0 if way > 0 else ys < n_y)
                    piece = index(zs, ys, c)
                    arrived(piece, here)
                    send(piece, UP_Y if way > 0 else DOWN_Y, here)
                    send(piece, CORE, here)

    def other_core(i, carry):
        forward(2 * i + 1 - c, CORE).wait_recv()
        return carry

    lax.fori_loop(0, n_rec // 2, other_core, 0)

    pair = 2 * rows_s

    def prepare(i, carry):
        s = jnp.concatenate([s_all[2 * i], s_all[2 * i + 1]], axis=0)
        hi, lo = split(s)
        s_cat[i] = jnp.concatenate([hi, lo, hi], axis=1)
        s_norm[i] = jnp.broadcast_to(jnp.sum(s * s, axis=1, keepdims=True), (pair, 128))
        return carry

    lax.fori_loop(0, n_rec // 2, prepare, 0)

    real = part[x_rows(n_feat), :]
    for q in range(1, n_feat):
        r_copies[q - 1].wait_recv()
        real = real + r_recv[q - 1]
    hi, lo = split(real)
    r_cat = jnp.concatenate([hi, hi, lo], axis=1)
    square = jnp.sum(real * real, axis=1, keepdims=True)
    r_norm = jnp.broadcast_to(square, (own, 128)).T[0:1, :]

    def send_min(i):
        peer = lax.rem(me + i, n_dev)
        to = peer // n_feat
        return pltpu.make_async_remote_copy(
            src_ref=min_send.at[to // 2], dst_ref=min_recv.at[me],
            send_sem=m_send.at[i], recv_sem=m_recv.at[me],
            device_id=(to, lax.rem(peer, n_feat)), device_id_type=MESH,
        )

    def recv_min(i):
        peer = lax.rem(me + i, n_dev)
        return pltpu.make_async_remote_copy(
            src_ref=min_send.at[0], dst_ref=min_recv.at[peer],
            send_sem=m_send.at[i], recv_sem=m_recv.at[peer],
            device_id=(peer // n_feat, lax.rem(peer, n_feat)), device_id_type=MESH,
        )

    best = jnp.full((1, own), jnp.inf, jnp.float32)
    for i in range(n_rec // 2):
        products = lax.dot_general(
            s_cat[i], r_cat, (((1,), (1,)), ((), ())), preferred_element_type=jnp.float32
        )
        dist = (s_norm[i][:, 0:1] + r_norm) - 2.0 * products
        best = jnp.minimum(best, jnp.min(dist, axis=0, keepdims=True))
        fold = dist[:, 0:128]
        for j in range(128, own, 128):
            fold = jnp.minimum(fold, dist[:, j : j + 128])
        min_send[i] = jnp.min(fold.T, axis=0, keepdims=True)

    rmin[f] = best / width

    def start_min(i, carry):
        send_min(i).start()
        return carry

    lax.fori_loop(1, n_dev, start_min, 0)

    def send_real(q, slot):
        return pltpu.make_async_remote_copy(
            src_ref=rmin.at[slot], dst_ref=rmin.at[slot],
            send_sem=o_send.at[q - 1], recv_sem=o_recv.at[q - 1],
            device_id=(r, lax.rem(f + q, n_feat)), device_id_type=MESH,
        )

    for q in range(1, n_feat):
        send_real(q, f).start()
    min_recv[me] = min_send[r // 2]

    for q in range(1, n_feat):
        send_real(q, lax.rem(f + n_feat - q, n_feat)).wait_recv()
    for q in range(n_feat):
        out_real[:, q * own : (q + 1) * own] = rmin[q]

    def wait_min(i, carry):
        recv_min(i).wait_recv()
        return carry

    lax.fori_loop(1, n_dev, wait_min, 0)
    least = jnp.min(min_recv[...], axis=0) / width
    out_synth[...] = jnp.where(c == 0, least[:, 0:rows_s], least[:, rows_s:pair])

    for q in range(1, n_feat):
        r_copies[q - 1].wait_send()
        send_real(q, f).wait_send()
    for piece, slot, when in sends:
        if when is None:
            forward(piece, slot).wait_send()
        else:
            pl.when(when)(functools.partial(lambda p, s: forward(p, s).wait_send(), piece, slot))

    def left_min(i, carry):
        send_min(i).wait_send()
        return carry

    lax.fori_loop(1, n_dev, left_min, 0)


def per_device(n_rec, n_feat, real, synth, proj):
    rows_r, genes = real.shape
    rows_s = synth.shape[0]
    width = proj.shape[1]
    own = rows_r // n_feat
    chips = n_rec // 2
    n_z = 1 << (chips.bit_length() // 2)
    n_y = chips // n_z
    n_k = 5
    n_dev = n_rec * n_feat
    f32, bf16 = jnp.float32, jnp.bfloat16
    dma = pltpu.SemaphoreType.DMA
    real_min, synth_min = pl.pallas_call(
        functools.partial(kernel, n_rec, n_feat, n_z, n_y, n_k),
        out_shape=(jax.ShapeDtypeStruct((1, rows_r), f32), jax.ShapeDtypeStruct((1, rows_s), f32)),
        in_specs=[pl.BlockSpec(memory_space=pl.ANY)] * 3,
        out_specs=(pl.BlockSpec(memory_space=pltpu.VMEM),) * 2,
        scratch_shapes=[
            pltpu.VMEM((rows_s + rows_r, genes), bf16),
            pltpu.VMEM((genes, width), bf16),
            pltpu.VMEM((rows_s + rows_r, width), f32),
            pltpu.VMEM((n_feat - 1, rows_s, width), f32),
            pltpu.VMEM((n_feat - 1, own, width), f32),
            pltpu.VMEM((n_rec, rows_s, width), f32),
            pltpu.VMEM((n_rec // 2, 2 * rows_s, 3 * width), bf16),
            pltpu.VMEM((n_rec // 2, 2 * rows_s, 128), f32),
            pltpu.VMEM((n_rec // 2, 1, 2 * rows_s), f32),
            pltpu.VMEM((n_dev, 1, 2 * rows_s), f32),
            pltpu.VMEM((n_feat, 1, own), f32),
            dma((n_k, 3)), dma((n_feat - 1,)),
            dma((n_feat - 1,)), dma((n_feat - 1,)), dma((n_feat - 1,)), dma((n_feat - 1,)),
            dma((n_rec, 5)), dma((n_rec,)),
            dma((n_dev,)), dma((n_dev,)), dma((n_feat - 1,)), dma((n_feat - 1,)),
        ],
        compiler_params=pltpu.CompilerParams(
            collective_id=0, has_side_effects=True, vmem_limit_bytes=56 * 1024 * 1024
        ),
        cost_estimate=pl.CostEstimate(
            flops=2 * (rows_r + rows_s) * genes * width + 6 * own * n_rec * rows_s * width,
            bytes_accessed=2 * genes * (rows_r + rows_s + width), transcendentals=0,
        ),
    )(real, synth, proj)
    return real_min.reshape(rows_r), synth_min.reshape(rows_s)


def solution(mesh):
    placed = (P("rec", "feat"), P("rec", "feat"), P("feat", None))
    body = functools.partial(per_device, mesh.shape["rec"], mesh.shape["feat"])
    return jax.shard_map(
        body, mesh=mesh, in_specs=placed, out_specs=(P("rec"), P("rec")), check_vma=False
    )
```

```python
import functools

import jax
import jax.numpy as jnp
from jax import lax
from jax.experimental import pallas as pl
from jax.experimental.pallas import tpu as pltpu
from jax.sharding import PartitionSpec as P

MESH = pl.DeviceIdType.MESH
UP_Z, DOWN_Z, UP_Y, DOWN_Y, CORE = range(5)
CUTS = 2


def split(x):
    hi = x.astype(jnp.bfloat16)
    lo = (x - hi.astype(jnp.float32)).astype(jnp.bfloat16)
    return hi, lo


def kernel(
    n_rec, n_feat, n_z, n_y, n_k,
    real_hbm, synth_hbm, proj_hbm, out_real, out_synth,
    x_v, proj_v, part, s_recv, r_recv, s_all, s_cat, s_norm, min_send, min_recv, rmin,
    in_sem, rest_sem, sx_send, sx_recv, rx_send, rx_recv, g_send, g_recv,
    m_send, m_recv, o_send, o_recv,
):
    r = lax.axis_index("rec")
    f = lax.axis_index("feat")
    c = lax.rem(r, 2)
    chip = r // 2
    y = lax.rem(chip, n_y)
    z = chip // n_y
    n_dev = n_rec * n_feat
    me = r * n_feat + f
    rows_s, genes = synth_hbm.shape
    rows_r = real_hbm.shape[0]
    width = proj_hbm.shape[1]
    own = rows_r // n_feat
    step = genes // n_k
    cut = rows_s // CUTS

    def chunk(q):
        start = lax.rem(f + q, n_feat) * own
        return pl.ds(pl.multiple_of(start, own), own)

    def x_rows(q):
        return pl.ds(rows_s + (q - 1) * own, own)

    loads = []
    for k in range(n_k):
        ks = pl.ds(k * step, step)
        loads.append([
            pltpu.make_async_copy(proj_hbm.at[ks], proj_v.at[ks], in_sem.at[k, 0]),
            pltpu.make_async_copy(synth_hbm.at[:, ks], x_v.at[pl.ds(0, rows_s), ks], in_sem.at[k, 1]),
            pltpu.make_async_copy(real_hbm.at[chunk(1), ks], x_v.at[x_rows(1), ks], in_sem.at[k, 2]),
        ])
        for copy in loads[-1]:
            copy.start()
    rest = []
    for q in range(2, n_feat + 1):
        rest.append(pltpu.make_async_copy(real_hbm.at[chunk(q)], x_v.at[x_rows(q)], rest_sem.at[q - 2]))
        rest[-1].start()

    barrier = pltpu.get_barrier_semaphore()

    def greet(i, carry):
        peer = lax.rem(me + i, n_dev)
        pl.semaphore_signal(
            barrier, inc=1, device_id=(peer // n_feat, lax.rem(peer, n_feat)), device_id_type=MESH
        )
        return carry

    lax.fori_loop(1, n_dev, greet, 0)

    head = rows_s + own
    for k in range(n_k):
        for copy in loads[k]:
            copy.wait()
        ks = pl.ds(k * step, step)
        term = jnp.dot(x_v[0:head, ks], proj_v[ks, :], preferred_element_type=jnp.float32)
        if k == 0:
            part[0:head, :] = term
        else:
            part[0:head, :] += term
    pl.semaphore_wait(barrier, n_dev - 1)

    s_copies, r_copies = [], []
    for q in range(1, n_feat):
        to = (r, lax.rem(f + q, n_feat))
        for h in range(CUTS):
            s_copies.append(pltpu.make_async_remote_copy(
                src_ref=part.at[pl.ds(h * cut, cut)], dst_ref=s_recv.at[q - 1, h],
                send_sem=sx_send.at[q - 1, h], recv_sem=sx_recv.at[q - 1, h],
                device_id=to, device_id_type=MESH,
            ))
            s_copies[-1].start()
        r_copies.append(pltpu.make_async_remote_copy(
            src_ref=part.at[x_rows(q)], dst_ref=r_recv.at[q - 1],
            send_sem=rx_send.at[q - 1], recv_sem=rx_recv.at[q - 1],
            device_id=to, device_id_type=MESH,
        ))
    for q in range(2, n_feat + 1):
        rest[q - 2].wait()
        part[x_rows(q), :] = jnp.dot(x_v[x_rows(q), :], proj_v[...], preferred_element_type=jnp.float32)
    for copy in s_copies:
        copy.wait_send()
    for copy in r_copies:
        copy.start()

    def index(zz, yy, cc):
        return (zz * n_y + yy) * 2 + cc

    def forward(piece, h, slot):
        to = {
            UP_Z: index(z + 1, y, c), DOWN_Z: index(z - 1, y, c),
            UP_Y: index(z, y + 1, c), DOWN_Y: index(z, y - 1, c), CORE: index(z, y, 1 - c),
        }[slot]
        return pltpu.make_async_remote_copy(
            src_ref=s_all.at[piece, h], dst_ref=s_all.at[piece, h],
            send_sem=g_send.at[piece, h, slot], recv_sem=g_recv.at[piece, h],
            device_id=(to, f), device_id_type=MESH,
        )

    exists = {UP_Z: z + 1 < n_z, DOWN_Z: z > 0, UP_Y: y + 1 < n_y, DOWN_Y: y > 0}
    always = z >= 0
    sends = []

    def send(piece, h, slots, when):
        for slot in slots:
            ok = jnp.logical_and(when, exists.get(slot, always))
            sends.append((piece, h, slot, ok))
            pl.when(ok)(functools.partial(lambda t: forward(piece, h, t).start(), slot))

    def arrived(piece, h, when):
        pl.when(when)(lambda: forward(piece, h, CORE).wait_recv())

    for wave in range(CUTS + n_z - 1):
        if wave < CUTS:
            total = part[wave * cut : (wave + 1) * cut, :]
            for q in range(1, n_feat):
                s_copies[(q - 1) * CUTS + wave].wait_recv()
                total = total + s_recv[q - 1, wave]
            s_all[r, wave] = total
            send(r, wave, (UP_Z, DOWN_Z, UP_Y, DOWN_Y, CORE), always)
        for d in range(1, n_z):
            h = wave - d
            if not 0 <= h < CUTS:
                continue
            for way in (1, -1):
                zs = z - way * d
                here = zs >= 0 if way > 0 else zs < n_z
                piece = index(zs, y, c)
                arrived(piece, h, here)
                send(piece, h, (UP_Z if way > 0 else DOWN_Z, UP_Y, DOWN_Y, CORE), here)

    pair = 2 * rows_s

    def prepare(i, when):
        def body():
            for h in range(CUTS):
                forward(2 * i + 1 - c, h, CORE).wait_recv()
            rows = jnp.concatenate(
                [s_all[2 * i].reshape(rows_s, width), s_all[2 * i + 1].reshape(rows_s, width)], axis=0
            )
            hi, lo = split(rows)
            s_cat[i] = jnp.concatenate([hi, lo, hi], axis=1)
            s_norm[i] = jnp.broadcast_to(jnp.sum(rows * rows, axis=1, keepdims=True), (pair, 128))

        pl.when(when)(body)

    todo = []
    order = [(zd, way) for zd in range(n_z) for way in (1, -1)[: 2 if zd else 1]]
    for zd, zway in order:
        zs = z - zway * zd
        z_ok = zs >= 0 if zway > 0 else zs < n_z
        todo.append((zs * n_y + y, z_ok))
    for d in range(1, n_y):
        for zd, zway in order:
            zs = z - zway * zd
            z_ok = zs >= 0 if zway > 0 else zs < n_z
            for way in (1, -1):
                ys = y - way * d
                here = jnp.logical_and(z_ok, ys >= 0 if way > 0 else ys < n_y)
                piece = index(zs, ys, c)
                for h in range(CUTS):
                    arrived(piece, h, here)
                    send(piece, h, (UP_Y if way > 0 else DOWN_Y, CORE), here)
                todo.append((zs * n_y + ys, here))
            if len(todo) > 2:
                prepare(*todo.pop(0))
    for item in todo:
        prepare(*item)

    real = part[x_rows(n_feat), :]
    for q in range(1, n_feat):
        r_copies[q - 1].wait_recv()
        real = real + r_recv[q - 1]
    hi, lo = split(real)
    r_cat = jnp.concatenate([hi, hi, lo], axis=1)
    square = jnp.sum(real * real, axis=1, keepdims=True)
    r_norm = jnp.broadcast_to(square, (own, 128)).T[0:1, :]

    def send_min(peer):
        to = peer // n_feat
        return pltpu.make_async_remote_copy(
            src_ref=min_send.at[to // 2], dst_ref=min_recv.at[me],
            send_sem=m_send.at[peer], recv_sem=m_recv.at[me],
            device_id=(to, lax.rem(peer, n_feat)), device_id_type=MESH,
        )

    def recv_min(peer):
        return pltpu.make_async_remote_copy(
            src_ref=min_send.at[0], dst_ref=min_recv.at[peer],
            send_sem=m_send.at[peer], recv_sem=m_recv.at[peer],
            device_id=(peer // n_feat, lax.rem(peer, n_feat)), device_id_type=MESH,
        )

    best = jnp.full((1, own), jnp.inf, jnp.float32)
    for b in range(n_rec // 4):
        products = lax.dot_general(
            s_cat[2 * b : 2 * b + 2].reshape(2 * pair, 3 * width), r_cat,
            (((1,), (1,)), ((), ())), preferred_element_type=jnp.float32,
        )
        norm = s_norm[2 * b : 2 * b + 2].reshape(2 * pair, 128)[:, 0:1]
        dist = (norm + r_norm) - 2.0 * products
        best = jnp.minimum(best, jnp.min(dist, axis=0, keepdims=True))
        fold = dist[:, 0:128]
        for j in range(128, own, 128):
            fold = jnp.minimum(fold, dist[:, j : j + 128])
        least = jnp.min(fold.T, axis=0, keepdims=True)
        min_send[2 * b] = least[:, 0:pair]
        min_send[2 * b + 1] = least[:, pair : 2 * pair]
        for peer in range(4 * b * n_feat, 4 * (b + 1) * n_feat):
            pl.when(peer != me)(functools.partial(lambda p: send_min(p).start(), peer))

    rmin[f] = best / width

    def send_real(q, slot):
        return pltpu.make_async_remote_copy(
            src_ref=rmin.at[slot], dst_ref=rmin.at[slot],
            send_sem=o_send.at[q - 1], recv_sem=o_recv.at[q - 1],
            device_id=(r, lax.rem(f + q, n_feat)), device_id_type=MESH,
        )

    for q in range(1, n_feat):
        send_real(q, f).start()
    min_recv[me] = min_send[r // 2]

    for q in range(1, n_feat):
        send_real(q, lax.rem(f + n_feat - q, n_feat)).wait_recv()
    for q in range(n_feat):
        out_real[:, q * own : (q + 1) * own] = rmin[q]

    def wait_min(i, carry):
        recv_min(lax.rem(me + i, n_dev)).wait_recv()
        return carry

    lax.fori_loop(1, n_dev, wait_min, 0)
    least = jnp.min(min_recv[...], axis=0) / width
    out_synth[...] = jnp.where(c == 0, least[:, 0:rows_s], least[:, rows_s:pair])

    for q in range(1, n_feat):
        r_copies[q - 1].wait_send()
        send_real(q, f).wait_send()
    for piece, h, slot, when in sends:
        pl.when(when)(functools.partial(lambda *t: forward(*t).wait_send(), piece, h, slot))

    def left_min(i, carry):
        send_min(lax.rem(me + i, n_dev)).wait_send()
        return carry

    lax.fori_loop(1, n_dev, left_min, 0)


def finish(real_ref, synth_ref, out_real, out_synth):
    out_real[...] = real_ref[...]
    out_synth[...] = synth_ref[...]


def per_device(n_rec, n_feat, real, synth, proj):
    rows_r, genes = real.shape
    rows_s = synth.shape[0]
    width = proj.shape[1]
    own = rows_r // n_feat
    chips = n_rec // 2
    n_z = 1 << (chips.bit_length() // 2)
    n_y = chips // n_z
    n_k = 5
    n_dev = n_rec * n_feat
    f32, bf16 = jnp.float32, jnp.bfloat16
    dma = pltpu.SemaphoreType.DMA
    real_min, synth_min = pl.pallas_call(
        functools.partial(kernel, n_rec, n_feat, n_z, n_y, n_k),
        out_shape=(jax.ShapeDtypeStruct((1, rows_r), f32), jax.ShapeDtypeStruct((1, rows_s), f32)),
        in_specs=[pl.BlockSpec(memory_space=pl.ANY)] * 3,
        out_specs=(pl.BlockSpec(memory_space=pltpu.VMEM),) * 2,
        scratch_shapes=[
            pltpu.VMEM((rows_s + rows_r, genes), bf16),
            pltpu.VMEM((genes, width), bf16),
            pltpu.VMEM((rows_s + rows_r, width), f32),
            pltpu.VMEM((n_feat - 1, CUTS, rows_s // CUTS, width), f32),
            pltpu.VMEM((n_feat - 1, own, width), f32),
            pltpu.VMEM((n_rec, CUTS, rows_s // CUTS, width), f32),
            pltpu.VMEM((n_rec // 2, 2 * rows_s, 3 * width), bf16),
            pltpu.VMEM((n_rec // 2, 2 * rows_s, 128), f32),
            pltpu.VMEM((n_rec // 2, 1, 2 * rows_s), f32),
            pltpu.VMEM((n_dev, 1, 2 * rows_s), f32),
            pltpu.VMEM((n_feat, 1, own), f32),
            dma((n_k, 3)), dma((n_feat - 1,)),
            dma((n_feat - 1, CUTS)), dma((n_feat - 1, CUTS)), dma((n_feat - 1,)), dma((n_feat - 1,)),
            dma((n_rec, CUTS, 5)), dma((n_rec, CUTS)),
            dma((n_dev,)), dma((n_dev,)), dma((n_feat - 1,)), dma((n_feat - 1,)),
        ],
        compiler_params=pltpu.CompilerParams(
            collective_id=0, has_side_effects=True, vmem_limit_bytes=56 * 1024 * 1024
        ),
        cost_estimate=pl.CostEstimate(
            flops=2 * (rows_r + rows_s) * genes * width + 6 * own * n_rec * rows_s * width,
            bytes_accessed=2 * genes * (rows_r + rows_s + width), transcendentals=0,
        ),
    )(real, synth, proj)
    real_min, synth_min = pl.pallas_call(
        finish,
        out_shape=(jax.ShapeDtypeStruct((1, rows_r), f32), jax.ShapeDtypeStruct((1, rows_s), f32)),
        in_specs=[pl.BlockSpec(memory_space=pltpu.VMEM)] * 2,
        out_specs=(pl.BlockSpec(memory_space=pltpu.VMEM),) * 2,
    )(real_min, synth_min)
    return real_min.reshape(rows_r), synth_min.reshape(rows_s)


def solution(mesh):
    placed = (P("rec", "feat"), P("rec", "feat"), P("feat", None))
    body = functools.partial(per_device, mesh.shape["rec"], mesh.shape["feat"])
    return jax.shard_map(
        body, mesh=mesh, in_specs=placed, out_specs=(P("rec"), P("rec")), check_vma=False
    )
```

```python
import functools

import jax
import jax.numpy as jnp
from jax import lax
from jax.experimental import pallas as pl
from jax.experimental.pallas import tpu as pltpu
from jax.sharding import PartitionSpec as P

MESH = pl.DeviceIdType.MESH
UP_Z, DOWN_Z, UP_Y, DOWN_Y, CORE = range(5)
CUTS = 2


def split(x):
    hi = x.astype(jnp.bfloat16)
    lo = (x - hi.astype(jnp.float32)).astype(jnp.bfloat16)
    return hi, lo


def kernel(
    n_rec, n_feat, n_z, n_y, n_k,
    real_hbm, synth_hbm, proj_hbm, out_real, out_synth,
    x_v, proj_v, part, s_recv, r_recv, s_all, s_cat, s_norm, min_send, min_recv, rmin,
    in_sem, rest_sem, sx_send, sx_recv, rx_send, rx_recv, g_send, g_recv,
    m_send, m_recv, o_send, o_recv,
):
    r = lax.axis_index("rec")
    f = lax.axis_index("feat")
    c = lax.rem(r, 2)
    chip = r // 2
    y = lax.rem(chip, n_y)
    z = chip // n_y
    n_dev = n_rec * n_feat
    me = r * n_feat + f
    rows_s, genes = synth_hbm.shape
    rows_r = real_hbm.shape[0]
    width = proj_hbm.shape[1]
    own = rows_r // n_feat
    step = genes // n_k
    cut = rows_s // CUTS

    def chunk(q):
        start = lax.rem(f + q, n_feat) * own
        return pl.ds(pl.multiple_of(start, own), own)

    def x_rows(q):
        return pl.ds(rows_s + (q - 1) * own, own)

    loads = []
    for k in range(n_k):
        ks = pl.ds(k * step, step)
        loads.append([
            pltpu.make_async_copy(proj_hbm.at[ks], proj_v.at[ks], in_sem.at[k, 0]),
            pltpu.make_async_copy(synth_hbm.at[:, ks], x_v.at[pl.ds(0, rows_s), ks], in_sem.at[k, 1]),
            pltpu.make_async_copy(real_hbm.at[chunk(1), ks], x_v.at[x_rows(1), ks], in_sem.at[k, 2]),
        ])
        for copy in loads[-1]:
            copy.start()
    rest = []
    for q in range(2, n_feat + 1):
        rest.append(pltpu.make_async_copy(real_hbm.at[chunk(q)], x_v.at[x_rows(q)], rest_sem.at[q - 2]))
        rest[-1].start()

    barrier = pltpu.get_barrier_semaphore()

    def greet(i, carry):
        peer = lax.rem(me + i, n_dev)
        pl.semaphore_signal(
            barrier, inc=1, device_id=(peer // n_feat, lax.rem(peer, n_feat)), device_id_type=MESH
        )
        return carry

    lax.fori_loop(1, n_dev, greet, 0)

    head = rows_s + own
    for k in range(n_k):
        for copy in loads[k]:
            copy.wait()
        ks = pl.ds(k * step, step)
        term = jnp.dot(x_v[0:head, ks], proj_v[ks, :], preferred_element_type=jnp.float32)
        if k == 0:
            part[0:head, :] = term
        else:
            part[0:head, :] += term
    pl.semaphore_wait(barrier, n_dev - 1)

    s_copies, r_copies = [], []
    for q in range(1, n_feat):
        to = (r, lax.rem(f + q, n_feat))
        for h in range(CUTS):
            s_copies.append(pltpu.make_async_remote_copy(
                src_ref=part.at[pl.ds(h * cut, cut)], dst_ref=s_recv.at[q - 1, h],
                send_sem=sx_send.at[q - 1, h], recv_sem=sx_recv.at[q - 1, h],
                device_id=to, device_id_type=MESH,
            ))
            s_copies[-1].start()
        r_copies.append(pltpu.make_async_remote_copy(
            src_ref=part.at[x_rows(q)], dst_ref=r_recv.at[q - 1],
            send_sem=rx_send.at[q - 1], recv_sem=rx_recv.at[q - 1],
            device_id=to, device_id_type=MESH,
        ))
    for q in range(2, n_feat + 1):
        rest[q - 2].wait()
        part[x_rows(q), :] = jnp.dot(x_v[x_rows(q), :], proj_v[...], preferred_element_type=jnp.float32)
    for copy in s_copies:
        copy.wait_send()
    for copy in r_copies:
        copy.start()

    def index(zz, yy, cc):
        return (zz * n_y + yy) * 2 + cc

    def forward(piece, h, slot):
        to = {
            UP_Z: index(z + 1, y, c), DOWN_Z: index(z - 1, y, c),
            UP_Y: index(z, y + 1, c), DOWN_Y: index(z, y - 1, c), CORE: index(z, y, 1 - c),
        }[slot]
        return pltpu.make_async_remote_copy(
            src_ref=s_all.at[piece, h], dst_ref=s_all.at[piece, h],
            send_sem=g_send.at[piece, h, slot], recv_sem=g_recv.at[piece, h],
            device_id=(to, f), device_id_type=MESH,
        )

    exists = {UP_Z: z + 1 < n_z, DOWN_Z: z > 0, UP_Y: y + 1 < n_y, DOWN_Y: y > 0}
    always = z >= 0
    sends = []

    def send(piece, h, slots, when):
        for slot in slots:
            ok = jnp.logical_and(when, exists.get(slot, always))
            sends.append((piece, h, slot, ok))
            pl.when(ok)(functools.partial(lambda t: forward(piece, h, t).start(), slot))

    def arrived(piece, h, when):
        pl.when(when)(lambda: forward(piece, h, CORE).wait_recv())

    for wave in range(CUTS + n_z - 1):
        if wave < CUTS:
            total = part[wave * cut : (wave + 1) * cut, :]
            for q in range(1, n_feat):
                s_copies[(q - 1) * CUTS + wave].wait_recv()
                total = total + s_recv[q - 1, wave]
            s_all[r, wave] = total
            send(r, wave, (UP_Z, DOWN_Z, UP_Y, DOWN_Y, CORE), always)
        for d in range(1, n_z):
            h = wave - d
            if not 0 <= h < CUTS:
                continue
            for way in (1, -1):
                zs = z - way * d
                here = zs >= 0 if way > 0 else zs < n_z
                piece = index(zs, y, c)
                arrived(piece, h, here)
                send(piece, h, (UP_Z if way > 0 else DOWN_Z, UP_Y, DOWN_Y, CORE), here)

    pair = 2 * rows_s

    def prepare(i, when):
        def body():
            for h in range(CUTS):
                forward(2 * i + 1 - c, h, CORE).wait_recv()
            rows = jnp.concatenate(
                [s_all[2 * i].reshape(rows_s, width), s_all[2 * i + 1].reshape(rows_s, width)], axis=0
            )
            hi, lo = split(rows)
            s_cat[i] = jnp.concatenate([hi, lo, hi], axis=1)
            s_norm[i] = jnp.broadcast_to(jnp.sum(rows * rows, axis=1, keepdims=True), (pair, 128))

        pl.when(when)(body)

    todo = []
    order = [(zd, way) for zd in range(n_z) for way in (1, -1)[: 2 if zd else 1]]
    for zd, zway in order:
        zs = z - zway * zd
        z_ok = zs >= 0 if zway > 0 else zs < n_z
        todo.append((zs * n_y + y, z_ok))
    for d in range(1, n_y):
        for zd, zway in order:
            zs = z - zway * zd
            z_ok = zs >= 0 if zway > 0 else zs < n_z
            for way in (1, -1):
                ys = y - way * d
                here = jnp.logical_and(z_ok, ys >= 0 if way > 0 else ys < n_y)
                piece = index(zs, ys, c)
                for h in range(CUTS):
                    arrived(piece, h, here)
                    send(piece, h, (UP_Y if way > 0 else DOWN_Y, CORE), here)
                todo.append((zs * n_y + ys, here))
            if len(todo) > 2:
                prepare(*todo.pop(0))
    for item in todo:
        prepare(*item)

    real = part[x_rows(n_feat), :]
    for q in range(1, n_feat):
        r_copies[q - 1].wait_recv()
        real = real + r_recv[q - 1]
    hi, lo = split(real)
    r_cat = jnp.concatenate([hi, hi, lo], axis=1)
    square = jnp.sum(real * real, axis=1, keepdims=True)
    r_norm = jnp.broadcast_to(square, (own, 128)).T[0:1, :]

    def send_min(peer):
        to = peer // n_feat
        return pltpu.make_async_remote_copy(
            src_ref=min_send.at[to // 2], dst_ref=min_recv.at[me],
            send_sem=m_send.at[peer], recv_sem=m_recv.at[me],
            device_id=(to, lax.rem(peer, n_feat)), device_id_type=MESH,
        )

    def recv_min(peer):
        return pltpu.make_async_remote_copy(
            src_ref=min_send.at[0], dst_ref=min_recv.at[peer],
            send_sem=m_send.at[peer], recv_sem=m_recv.at[peer],
            device_id=(peer // n_feat, lax.rem(peer, n_feat)), device_id_type=MESH,
        )

    best = jnp.full((1, own), jnp.inf, jnp.float32)
    for b in range(n_rec // 4):
        products = lax.dot_general(
            s_cat[2 * b : 2 * b + 2].reshape(2 * pair, 3 * width), r_cat,
            (((1,), (1,)), ((), ())), preferred_element_type=jnp.float32,
        )
        norm = s_norm[2 * b : 2 * b + 2].reshape(2 * pair, 128)[:, 0:1]
        dist = (norm + r_norm) - 2.0 * products
        best = jnp.minimum(best, jnp.min(dist, axis=0, keepdims=True))
        fold = dist[:, 0:128]
        for j in range(128, own, 128):
            fold = jnp.minimum(fold, dist[:, j : j + 128])
        least = jnp.min(fold.T, axis=0, keepdims=True)
        min_send[2 * b] = least[:, 0:pair]
        min_send[2 * b + 1] = least[:, pair : 2 * pair]
        for peer in range(4 * b * n_feat, 4 * (b + 1) * n_feat):
            pl.when(peer != me)(functools.partial(lambda p: send_min(p).start(), peer))

    rmin[f] = best / width

    def send_real(q, slot):
        return pltpu.make_async_remote_copy(
            src_ref=rmin.at[slot], dst_ref=rmin.at[slot],
            send_sem=o_send.at[q - 1], recv_sem=o_recv.at[q - 1],
            device_id=(r, lax.rem(f + q, n_feat)), device_id_type=MESH,
        )

    for q in range(1, n_feat):
        send_real(q, f).start()
    min_recv[me] = min_send[r // 2]

    for q in range(1, n_feat):
        r_copies[q - 1].wait_send()
        send_real(q, f).wait_send()
    for piece, h, slot, when in sends:
        pl.when(when)(functools.partial(lambda *t: forward(*t).wait_send(), piece, h, slot))

    def left_min(i, carry):
        send_min(lax.rem(me + i, n_dev)).wait_send()
        return carry

    lax.fori_loop(1, n_dev, left_min, 0)

    for q in range(1, n_feat):
        send_real(q, lax.rem(f + n_feat - q, n_feat)).wait_recv()
    for q in range(n_feat):
        out_real[:, q * own : (q + 1) * own] = rmin[q]

    def wait_min(i, carry):
        recv_min(lax.rem(me + i, n_dev)).wait_recv()
        return carry

    lax.fori_loop(1, n_dev, wait_min, 0)
    least = jnp.min(min_recv[...], axis=0) / width
    out_synth[...] = jnp.where(c == 0, least[:, 0:rows_s], least[:, rows_s:pair])


def finish(real_ref, synth_ref, out_real, out_synth):
    out_real[...] = real_ref[...]
    out_synth[...] = synth_ref[...]


def per_device(n_rec, n_feat, real, synth, proj):
    rows_r, genes = real.shape
    rows_s = synth.shape[0]
    width = proj.shape[1]
    own = rows_r // n_feat
    chips = n_rec // 2
    n_z = 1 << (chips.bit_length() // 2)
    n_y = chips // n_z
    n_k = 5
    n_dev = n_rec * n_feat
    f32, bf16 = jnp.float32, jnp.bfloat16
    dma = pltpu.SemaphoreType.DMA
    real_min, synth_min = pl.pallas_call(
        functools.partial(kernel, n_rec, n_feat, n_z, n_y, n_k),
        out_shape=(jax.ShapeDtypeStruct((1, rows_r), f32), jax.ShapeDtypeStruct((1, rows_s), f32)),
        in_specs=[pl.BlockSpec(memory_space=pl.ANY)] * 3,
        out_specs=(pl.BlockSpec(memory_space=pltpu.VMEM),) * 2,
        scratch_shapes=[
            pltpu.VMEM((rows_s + rows_r, genes), bf16),
            pltpu.VMEM((genes, width), bf16),
            pltpu.VMEM((rows_s + rows_r, width), f32),
            pltpu.VMEM((n_feat - 1, CUTS, rows_s // CUTS, width), f32),
            pltpu.VMEM((n_feat - 1, own, width), f32),
            pltpu.VMEM((n_rec, CUTS, rows_s // CUTS, width), f32),
            pltpu.VMEM((n_rec // 2, 2 * rows_s, 3 * width), bf16),
            pltpu.VMEM((n_rec // 2, 2 * rows_s, 128), f32),
            pltpu.VMEM((n_rec // 2, 1, 2 * rows_s), f32),
            pltpu.VMEM((n_dev, 1, 2 * rows_s), f32),
            pltpu.VMEM((n_feat, 1, own), f32),
            dma((n_k, 3)), dma((n_feat - 1,)),
            dma((n_feat - 1, CUTS)), dma((n_feat - 1, CUTS)), dma((n_feat - 1,)), dma((n_feat - 1,)),
            dma((n_rec, CUTS, 5)), dma((n_rec, CUTS)),
            dma((n_dev,)), dma((n_dev,)), dma((n_feat - 1,)), dma((n_feat - 1,)),
        ],
        compiler_params=pltpu.CompilerParams(
            collective_id=0, has_side_effects=True, vmem_limit_bytes=56 * 1024 * 1024
        ),
        cost_estimate=pl.CostEstimate(
            flops=2 * (rows_r + rows_s) * genes * width + 6 * own * n_rec * rows_s * width,
            bytes_accessed=2 * genes * (rows_r + rows_s + width), transcendentals=0,
        ),
    )(real, synth, proj)
    real_min, synth_min = pl.pallas_call(
        finish,
        out_shape=(jax.ShapeDtypeStruct((1, rows_r), f32), jax.ShapeDtypeStruct((1, rows_s), f32)),
        in_specs=[pl.BlockSpec(memory_space=pltpu.VMEM)] * 2,
        out_specs=(pl.BlockSpec(memory_space=pltpu.VMEM),) * 2,
    )(real_min, synth_min)
    return real_min.reshape(rows_r), synth_min.reshape(rows_s)


def solution(mesh):
    placed = (P("rec", "feat"), P("rec", "feat"), P("feat", None))
    body = functools.partial(per_device, mesh.shape["rec"], mesh.shape["feat"])
    return jax.shard_map(
        body, mesh=mesh, in_specs=placed, out_specs=(P("rec"), P("rec")), check_vma=False
    )
```

```python
import functools

import jax
import jax.numpy as jnp
from jax import lax
from jax.experimental import pallas as pl
from jax.experimental.pallas import tpu as pltpu
from jax.sharding import PartitionSpec as P

MESH = pl.DeviceIdType.MESH
UP_Z, DOWN_Z, UP_Y, DOWN_Y, CORE = range(5)
CUTS = 2


def split(x):
    hi = x.astype(jnp.bfloat16)
    lo = (x - hi.astype(jnp.float32)).astype(jnp.bfloat16)
    return hi, lo


def kernel(
    n_rec, n_feat, n_z, n_y, n_k,
    real_hbm, synth_hbm, proj_hbm, out_real, out_synth,
    x_v, proj_v, part, s_recv, r_recv, s_all, s_cat, s_norm, min_send, min_recv, rmin,
    in_sem, rest_sem, sx_send, sx_recv, rx_send, rx_recv, g_send, g_recv,
    m_send, m_recv, o_send, o_recv,
):
    r = lax.axis_index("rec")
    f = lax.axis_index("feat")
    c = lax.rem(r, 2)
    chip = r // 2
    y = lax.rem(chip, n_y)
    z = chip // n_y
    n_dev = n_rec * n_feat
    me = r * n_feat + f
    rows_s, genes = synth_hbm.shape
    rows_r = real_hbm.shape[0]
    width = proj_hbm.shape[1]
    own = rows_r // n_feat
    step = genes // n_k
    cut = rows_s // CUTS

    def chunk(q):
        start = lax.rem(f + q, n_feat) * own
        return pl.ds(pl.multiple_of(start, own), own)

    def x_rows(q):
        return pl.ds(rows_s + (q - 1) * own, own)

    loads = []
    for k in range(n_k):
        ks = pl.ds(k * step, step)
        loads.append([
            pltpu.make_async_copy(proj_hbm.at[ks], proj_v.at[ks], in_sem.at[k, 0]),
            pltpu.make_async_copy(synth_hbm.at[:, ks], x_v.at[pl.ds(0, rows_s), ks], in_sem.at[k, 1]),
            pltpu.make_async_copy(real_hbm.at[chunk(1), ks], x_v.at[x_rows(1), ks], in_sem.at[k, 2]),
        ])
        for copy in loads[-1]:
            copy.start()
    rest = []
    for q in range(2, n_feat + 1):
        rest.append(pltpu.make_async_copy(real_hbm.at[chunk(q)], x_v.at[x_rows(q)], rest_sem.at[q - 2]))
        rest[-1].start()

    barrier = pltpu.get_barrier_semaphore()

    def greet(i, carry):
        peer = lax.rem(me + i, n_dev)
        pl.semaphore_signal(
            barrier, inc=1, device_id=(peer // n_feat, lax.rem(peer, n_feat)), device_id_type=MESH
        )
        return carry

    lax.fori_loop(1, n_dev, greet, 0)

    head = rows_s + own
    for k in range(n_k):
        for copy in loads[k]:
            copy.wait()
        ks = pl.ds(k * step, step)
        term = jnp.dot(x_v[0:head, ks], proj_v[ks, :], preferred_element_type=jnp.float32)
        if k == 0:
            part[0:head, :] = term
        else:
            part[0:head, :] += term
    pl.semaphore_wait(barrier, n_dev - 1)

    s_copies, r_copies = [], []
    for q in range(1, n_feat):
        to = (r, lax.rem(f + q, n_feat))
        for h in range(CUTS):
            s_copies.append(pltpu.make_async_remote_copy(
                src_ref=part.at[pl.ds(h * cut, cut)], dst_ref=s_recv.at[q - 1, h],
                send_sem=sx_send.at[q - 1, h], recv_sem=sx_recv.at[q - 1, h],
                device_id=to, device_id_type=MESH,
            ))
            s_copies[-1].start()
        r_copies.append(pltpu.make_async_remote_copy(
            src_ref=part.at[x_rows(q)], dst_ref=r_recv.at[q - 1],
            send_sem=rx_send.at[q - 1], recv_sem=rx_recv.at[q - 1],
            device_id=to, device_id_type=MESH,
        ))
    for q in range(2, n_feat + 1):
        rest[q - 2].wait()
        part[x_rows(q), :] = jnp.dot(x_v[x_rows(q), :], proj_v[...], preferred_element_type=jnp.float32)
    for copy in s_copies:
        copy.wait_send()
    for copy in r_copies:
        copy.start()

    def index(zz, yy, cc):
        return (zz * n_y + yy) * 2 + cc

    def forward(piece, h, slot):
        to = {
            UP_Z: index(z + 1, y, c), DOWN_Z: index(z - 1, y, c),
            UP_Y: index(z, y + 1, c), DOWN_Y: index(z, y - 1, c), CORE: index(z, y, 1 - c),
        }[slot]
        return pltpu.make_async_remote_copy(
            src_ref=s_all.at[piece, h], dst_ref=s_all.at[piece, h],
            send_sem=g_send.at[piece, h, slot], recv_sem=g_recv.at[piece, h],
            device_id=(to, f), device_id_type=MESH,
        )

    exists = {UP_Z: z + 1 < n_z, DOWN_Z: z > 0, UP_Y: y + 1 < n_y, DOWN_Y: y > 0}
    always = z >= 0
    sends = []

    def send(piece, h, slots, when):
        for slot in slots:
            ok = jnp.logical_and(when, exists.get(slot, always))
            sends.append((piece, h, slot, ok))
            pl.when(ok)(functools.partial(lambda t: forward(piece, h, t).start(), slot))

    def arrived(piece, h, when):
        pl.when(when)(lambda: forward(piece, h, CORE).wait_recv())

    for wave in range(CUTS + n_z - 1):
        if wave < CUTS:
            total = part[wave * cut : (wave + 1) * cut, :]
            for q in range(1, n_feat):
                s_copies[(q - 1) * CUTS + wave].wait_recv()
                total = total + s_recv[q - 1, wave]
            s_all[r, wave] = total
            send(r, wave, (UP_Z, DOWN_Z, UP_Y, DOWN_Y, CORE), always)
        for d in range(1, n_z):
            h = wave - d
            if not 0 <= h < CUTS:
                continue
            for way in (1, -1):
                zs = z - way * d
                here = zs >= 0 if way > 0 else zs < n_z
                piece = index(zs, y, c)
                arrived(piece, h, here)
                send(piece, h, (UP_Z if way > 0 else DOWN_Z, UP_Y, DOWN_Y, CORE), here)

    pair = 2 * rows_s

    def prepare(i, when):
        def body():
            for h in range(CUTS):
                forward(2 * i + 1 - c, h, CORE).wait_recv()
            rows = jnp.concatenate(
                [s_all[2 * i].reshape(rows_s, width), s_all[2 * i + 1].reshape(rows_s, width)], axis=0
            )
            hi, lo = split(rows)
            s_cat[i] = jnp.concatenate([hi, lo, hi], axis=1)
            s_norm[i] = jnp.broadcast_to(jnp.sum(rows * rows, axis=1, keepdims=True), (pair, 128))

        pl.when(when)(body)

    todo = []
    order = [(zd, way) for zd in range(n_z) for way in (1, -1)[: 2 if zd else 1]]
    for zd, zway in order:
        zs = z - zway * zd
        z_ok = zs >= 0 if zway > 0 else zs < n_z
        todo.append((zs * n_y + y, z_ok))
    for d in range(1, n_y):
        for zd, zway in order:
            zs = z - zway * zd
            z_ok = zs >= 0 if zway > 0 else zs < n_z
            for way in (1, -1):
                ys = y - way * d
                here = jnp.logical_and(z_ok, ys >= 0 if way > 0 else ys < n_y)
                piece = index(zs, ys, c)
                for h in range(CUTS):
                    arrived(piece, h, here)
                    send(piece, h, (UP_Y if way > 0 else DOWN_Y, CORE), here)
                todo.append((zs * n_y + ys, here))
            if len(todo) > 2:
                prepare(*todo.pop(0))
    real = part[x_rows(n_feat), :]
    for q in range(1, n_feat):
        r_copies[q - 1].wait_recv()
        real = real + r_recv[q - 1]
    hi, lo = split(real)
    r_cat = jnp.concatenate([hi, hi, lo], axis=1)
    square = jnp.sum(real * real, axis=1, keepdims=True)
    r_norm = jnp.broadcast_to(square, (own, 128)).T[0:1, :]

    for item in todo:
        prepare(*item)

    def send_min(peer):
        to = peer // n_feat
        return pltpu.make_async_remote_copy(
            src_ref=min_send.at[to // 2], dst_ref=min_recv.at[me],
            send_sem=m_send.at[peer], recv_sem=m_recv.at[me],
            device_id=(to, lax.rem(peer, n_feat)), device_id_type=MESH,
        )

    def recv_min(peer):
        return pltpu.make_async_remote_copy(
            src_ref=min_send.at[0], dst_ref=min_recv.at[peer],
            send_sem=m_send.at[peer], recv_sem=m_recv.at[peer],
            device_id=(peer // n_feat, lax.rem(peer, n_feat)), device_id_type=MESH,
        )

    best = jnp.full((1, own), jnp.inf, jnp.float32)
    for b in range(n_rec // 4):
        products = lax.dot_general(
            s_cat[2 * b : 2 * b + 2].reshape(2 * pair, 3 * width), r_cat,
            (((1,), (1,)), ((), ())), preferred_element_type=jnp.float32,
        )
        norm = s_norm[2 * b : 2 * b + 2].reshape(2 * pair, 128)[:, 0:1]
        dist = (norm + r_norm) - 2.0 * products
        best = jnp.minimum(best, jnp.min(dist, axis=0, keepdims=True))
        fold = dist[:, 0:128]
        for j in range(128, own, 128):
            fold = jnp.minimum(fold, dist[:, j : j + 128])
        least = jnp.min(fold.T, axis=0, keepdims=True)
        min_send[2 * b] = least[:, 0:pair]
        min_send[2 * b + 1] = least[:, pair : 2 * pair]
        for peer in range(4 * b * n_feat, 4 * (b + 1) * n_feat):
            pl.when(peer != me)(functools.partial(lambda p: send_min(p).start(), peer))

    rmin[f] = best / width

    def send_real(q, slot):
        return pltpu.make_async_remote_copy(
            src_ref=rmin.at[slot], dst_ref=rmin.at[slot],
            send_sem=o_send.at[q - 1], recv_sem=o_recv.at[q - 1],
            device_id=(r, lax.rem(f + q, n_feat)), device_id_type=MESH,
        )

    for q in range(1, n_feat):
        send_real(q, f).start()
    min_recv[me] = min_send[r // 2]

    for q in range(1, n_feat):
        r_copies[q - 1].wait_send()
        send_real(q, f).wait_send()
    for piece, h, slot, when in sends:
        pl.when(when)(functools.partial(lambda *t: forward(*t).wait_send(), piece, h, slot))

    def left_min(i, carry):
        send_min(lax.rem(me + i, n_dev)).wait_send()
        return carry

    lax.fori_loop(1, n_dev, left_min, 0)

    for q in range(1, n_feat):
        send_real(q, lax.rem(f + n_feat - q, n_feat)).wait_recv()
    for q in range(n_feat):
        out_real[:, q * own : (q + 1) * own] = rmin[q]

    def wait_min(i, carry):
        recv_min(lax.rem(me + i, n_dev)).wait_recv()
        return carry

    lax.fori_loop(1, n_dev, wait_min, 0)
    least = jnp.min(min_recv[...], axis=0) / width
    out_synth[...] = jnp.where(c == 0, least[:, 0:rows_s], least[:, rows_s:pair])


def finish(real_ref, synth_ref, out_real, out_synth):
    out_real[...] = real_ref[...]
    out_synth[...] = synth_ref[...]


def per_device(n_rec, n_feat, real, synth, proj):
    rows_r, genes = real.shape
    rows_s = synth.shape[0]
    width = proj.shape[1]
    own = rows_r // n_feat
    chips = n_rec // 2
    n_z = 1 << (chips.bit_length() // 2)
    n_y = chips // n_z
    n_k = 5
    n_dev = n_rec * n_feat
    f32, bf16 = jnp.float32, jnp.bfloat16
    dma = pltpu.SemaphoreType.DMA
    real_min, synth_min = pl.pallas_call(
        functools.partial(kernel, n_rec, n_feat, n_z, n_y, n_k),
        out_shape=(jax.ShapeDtypeStruct((1, rows_r), f32), jax.ShapeDtypeStruct((1, rows_s), f32)),
        in_specs=[pl.BlockSpec(memory_space=pl.ANY)] * 3,
        out_specs=(pl.BlockSpec(memory_space=pltpu.VMEM),) * 2,
        scratch_shapes=[
            pltpu.VMEM((rows_s + rows_r, genes), bf16),
            pltpu.VMEM((genes, width), bf16),
            pltpu.VMEM((rows_s + rows_r, width), f32),
            pltpu.VMEM((n_feat - 1, CUTS, rows_s // CUTS, width), f32),
            pltpu.VMEM((n_feat - 1, own, width), f32),
            pltpu.VMEM((n_rec, CUTS, rows_s // CUTS, width), f32),
            pltpu.VMEM((n_rec // 2, 2 * rows_s, 3 * width), bf16),
            pltpu.VMEM((n_rec // 2, 2 * rows_s, 128), f32),
            pltpu.VMEM((n_rec // 2, 1, 2 * rows_s), f32),
            pltpu.VMEM((n_dev, 1, 2 * rows_s), f32),
            pltpu.VMEM((n_feat, 1, own), f32),
            dma((n_k, 3)), dma((n_feat - 1,)),
            dma((n_feat - 1, CUTS)), dma((n_feat - 1, CUTS)), dma((n_feat - 1,)), dma((n_feat - 1,)),
            dma((n_rec, CUTS, 5)), dma((n_rec, CUTS)),
            dma((n_dev,)), dma((n_dev,)), dma((n_feat - 1,)), dma((n_feat - 1,)),
        ],
        compiler_params=pltpu.CompilerParams(
            collective_id=0, has_side_effects=True, vmem_limit_bytes=56 * 1024 * 1024
        ),
        cost_estimate=pl.CostEstimate(
            flops=2 * (rows_r + rows_s) * genes * width + 6 * own * n_rec * rows_s * width,
            bytes_accessed=2 * genes * (rows_r + rows_s + width), transcendentals=0,
        ),
    )(real, synth, proj)
    real_min, synth_min = pl.pallas_call(
        finish,
        out_shape=(jax.ShapeDtypeStruct((1, rows_r), f32), jax.ShapeDtypeStruct((1, rows_s), f32)),
        in_specs=[pl.BlockSpec(memory_space=pltpu.VMEM)] * 2,
        out_specs=(pl.BlockSpec(memory_space=pltpu.VMEM),) * 2,
    )(real_min, synth_min)
    return real_min.reshape(rows_r), synth_min.reshape(rows_s)


def solution(mesh):
    placed = (P("rec", "feat"), P("rec", "feat"), P("feat", None))
    body = functools.partial(per_device, mesh.shape["rec"], mesh.shape["feat"])
    return jax.shard_map(
        body, mesh=mesh, in_specs=placed, out_specs=(P("rec"), P("rec")), check_vma=False
    )
```
